256 devices in a mesh: gx: 32 (over z, x), gy: 8 (over y, core).
Axes of the slice: x: 4, y: 4, z: 8, core: 2. Of those that a mesh axis runs over, the one named last changes fastest.
Arguments:
- occupied: bfloat16 [32, 128, 128, 256], P(None, 'gx', 'gy'), as said below
- search_dirs: bfloat16 [32, 128, 128, 256], P(None, 'gx', 'gy'), as said below
- previous_dirs: bfloat16 [32, 128, 128, 256], P(None, 'gx', 'gy'), as said below
- occupied_image: bfloat16 [32, 128, 128, 256], P(None, 'gx', 'gy'), as said below
- previous_image: bfloat16 [32, 128, 128, 256], P(None, 'gx', 'gy'), as said below
- potential: float32 [128, 128, 256], P('gx', 'gy'), may hold values from -18 to 0, as said below
- ritz_vectors: bfloat16 [96, 32], replicated, may hold values from -3 to 3, as said below
Outputs:
- new_block: bfloat16 [32, 128, 128, 256], P(None, 'gx', 'gy')
- ritz_matrix: float32 [32, 32], replicated
- search_image: bfloat16 [32, 128, 128, 256], P(None, 'gx', 'gy')
The draws below stay inside these ranges and needn't reach their ends.
Inputs may be any that keep to these rules, and one draw needn't show every extreme that they name: `occupied`: orbital fields of order 1 / sqrt(4194304) a cell. `search_dirs`: orbital fields of order 1 / sqrt(4194304) a cell. `previous_dirs`: orbital fields of order 1 / sqrt(4194304) a cell. `occupied_image`: fields of order a few / sqrt(4194304) a cell. `previous_image`: fields of order a few / sqrt(4194304) a cell. `potential`: non-positive. `ritz_vectors`: the correlation of the new block is positive definite.
All inputs are finite; a program needn't handle non-finite values.
Results may differ from the reference program's by a relative error of at most 0.002.
Values may be sent and summed in bfloat16 or wider, within the bound.
A program may use at most 128 MiB of HBM per device.

```python
import math
import jax
import jax.numpy as jnp
from jax import lax

ORB = 32
BASIS = 96
NX = 128
NY = 128
NZ = 256


def wave_phase(wave_numbers, length, position_shape):
    cells = jnp.arange(length, dtype=jnp.int32).reshape(position_shape)
    return (wave_numbers * cells % length).astype(jnp.float32) / float(length)


def smooth_field(key):
    waves = 6
    keys = jax.random.split(key, 5)
    limit_x = max(NX // 6, 1)
    limit_y = max(NY // 6, 1)
    limit_z = max(NZ // 6, 1)
    wave_x = jax.random.randint(keys[0], (waves, ORB, 1, 1, 1), -limit_x, limit_x + 1, jnp.int32)
    wave_y = jax.random.randint(keys[1], (waves, ORB, 1, 1, 1), -limit_y, limit_y + 1, jnp.int32)
    wave_z = jax.random.randint(keys[2], (waves, ORB, 1, 1, 1), -limit_z, limit_z + 1, jnp.int32)
    offsets = jax.random.uniform(keys[3], (waves, ORB, 1, 1, 1), jnp.float32, 0.0, 1.0)
    gauss_amp = jax.random.truncated_normal(keys[4], -4.0, 4.0, (waves, ORB, 1, 1, 1), jnp.float32)
    amplitude = gauss_amp
    total = jnp.zeros((ORB, NX, NY, NZ), jnp.float32)
    for wave in range(waves):
        phase = wave_phase(wave_x[wave], NX, (1, NX, 1, 1))
        phase = phase + wave_phase(wave_y[wave], NY, (1, 1, NY, 1))
        phase = phase + wave_phase(wave_z[wave], NZ, (1, 1, 1, NZ))
        total = total + amplitude[wave] * jnp.cos(2.0 * math.pi * (phase + offsets[wave]))
    return total * math.sqrt(2.0 / waves)


def orbital_field(key, constant):
    key = jax.random.fold_in(key, constant)
    first = jax.random.fold_in(key, 0)
    fourth = jax.random.fold_in(key, 3)
    shape = (ORB, NX, NY, NZ)
    gauss = jax.random.truncated_normal(first, -4.0, 4.0, shape, jnp.float32)
    rough = gauss
    values = 0.8 * smooth_field(fourth) + 0.6 * rough
    position = jnp.arange(NX, dtype=jnp.float32).reshape(1, NX, 1, 1) / max(NX - 1, 1)
    envelope = 1.0 + 2.0 * position
    return values * envelope * (0.48 / math.sqrt(NX * NY * NZ))


def image_of(key, constant):
    shared = orbital_field(key, constant)
    key = jax.random.fold_in(key, constant + 100)
    level_key, jitter_key = jax.random.split(key)
    levels = jax.random.uniform(level_key, (ORB, 1, 1, 1), jnp.float32, -3.0, 1.0)
    jitter = orbital_field(jitter_key, constant + 200)
    return levels * shared + 0.5 * jitter


def draw_occupied(key, part):
    return orbital_field(key, 11).astype(jnp.bfloat16)


def draw_occupied_image(key, part):
    return image_of(key, 11).astype(jnp.bfloat16)


def draw_previous_dirs(key, part):
    return orbital_field(key, 12).astype(jnp.bfloat16)


def draw_previous_image(key, part):
    return image_of(key, 12).astype(jnp.bfloat16)


def draw_search_dirs(key, part):
    return orbital_field(key, 13).astype(jnp.bfloat16)


def draw_potential(key, part):
    key = jax.random.fold_in(key, 7)
    depth_key, rough_key = jax.random.split(key)
    depth = jnp.exp(jax.random.uniform(depth_key, (NX, 1, 1), jnp.float32, math.log(0.5), math.log(12.0)))
    rough = jax.random.uniform(rough_key, (NX, NY, NZ), jnp.float32, 0.5, 1.5)
    return -depth * rough


def draw_ritz_vectors(key, part):
    key = jax.random.fold_in(key, 5)
    rows = jnp.arange(BASIS, dtype=jnp.int32).reshape(BASIS, 1)
    columns = jnp.arange(ORB, dtype=jnp.int32).reshape(1, ORB)
    identity = jnp.where(rows == columns, 1.0, 0.0).astype(jnp.float32)
    return (identity + 0.3 * jax.random.truncated_normal(key, -4.0, 4.0, (BASIS, ORB), jnp.float32)).astype(jnp.bfloat16)


def setup_inputs(seed: int = 0) -> dict:
    key_of = jax.random.split(jax.random.key(seed), 8)
    occupied = draw_occupied(jax.random.fold_in(key_of[7], 71), 0)
    search_dirs = draw_search_dirs(jax.random.fold_in(key_of[7], 71), 0)
    previous_dirs = draw_previous_dirs(jax.random.fold_in(key_of[7], 71), 0)
    occupied_image = draw_occupied_image(jax.random.fold_in(key_of[7], 71), 0)
    previous_image = draw_previous_image(jax.random.fold_in(key_of[7], 71), 0)
    potential = draw_potential(jax.random.fold_in(key_of[7], 71), 0)
    ritz_vectors = draw_ritz_vectors(jax.random.fold_in(key_of[7], 71), 0)
    return {"occupied": occupied, "search_dirs": search_dirs, "previous_dirs": previous_dirs, "occupied_image": occupied_image, "previous_image": previous_image, "potential": potential, "ritz_vectors": ritz_vectors}


COEFFS = (-205.0 / 72.0, 8.0 / 5.0, -1.0 / 5.0, 8.0 / 315.0, -1.0 / 560.0)

def laplacian(values):
    summed = 3.0 * COEFFS[0] * values
    for dimension in (0, 1, 2):
        for offset in range(1, 5):
            paired = jnp.roll(values, offset, dimension) + jnp.roll(values, -offset, dimension)
            summed = summed + COEFFS[offset] * paired
    return summed

def contract(left_rows, right_rows):
    return lax.dot_general(left_rows.astype(jnp.float32), right_rows.astype(jnp.float32), (((1,), (1,)), ((), ())), preferred_element_type=jnp.float32)

def reference(occupied, search_dirs, previous_dirs, occupied_image, previous_image, potential, ritz_vectors):

    def kinetic(orbital):
        values = orbital.astype(jnp.float32)
        return (-0.5 * laplacian(values) + potential * values).astype(jnp.bfloat16)
    search_image = lax.map(kinetic, search_dirs)
    blocks = [occupied.reshape(ORB, -1), search_dirs.reshape(ORB, -1), previous_dirs.reshape(ORB, -1)]
    images = [occupied_image.reshape(ORB, -1), search_image.reshape(ORB, -1), previous_image.reshape(ORB, -1)]
    gram_correlation = jnp.concatenate([jnp.concatenate([contract(first, second) for second in blocks], 1) for first in blocks], 0)
    gram_energy = jnp.concatenate([jnp.concatenate([contract(first, second) for second in images], 1) for first in blocks], 0)
    coeff_float = ritz_vectors.astype(jnp.float32)
    highest = lax.Precision.HIGHEST
    proj_correlation = jnp.dot(coeff_float.T, jnp.dot(gram_correlation, coeff_float, precision=highest), precision=highest)
    proj_energy = jnp.dot(coeff_float.T, jnp.dot(gram_energy, coeff_float, precision=highest), precision=highest)
    factor = jnp.linalg.cholesky(proj_correlation)
    half_solved = lax.linalg.triangular_solve(factor, proj_energy, left_side=True, lower=True)
    ritz_matrix = lax.linalg.triangular_solve(factor, half_solved.T, left_side=True, lower=True).T
    rotated = jnp.dot(ritz_vectors[0:ORB].T.astype(jnp.float32), blocks[0].astype(jnp.float32), preferred_element_type=jnp.float32)
    rotated = rotated + jnp.dot(ritz_vectors[ORB:2 * ORB].T.astype(jnp.float32), blocks[1].astype(jnp.float32), preferred_element_type=jnp.float32)
    rotated = rotated + jnp.dot(ritz_vectors[2 * ORB:3 * ORB].T.astype(jnp.float32), blocks[2].astype(jnp.float32), preferred_element_type=jnp.float32)
    new_block = lax.linalg.triangular_solve(factor, rotated, left_side=True, lower=True)
    new_block = new_block.astype(jnp.bfloat16).reshape(ORB, NX, NY, NZ)
    return (new_block, ritz_matrix, search_image)
```

```python
import itertools

import jax
import jax.numpy as jnp
import ml_dtypes
import numpy as np
from jax import lax
from jax.experimental import pallas as pl
from jax.experimental.pallas import tpu as pltpu
from jax.sharding import PartitionSpec as P

MESH = pl.DeviceIdType.MESH
HIGHEST = lax.Precision.HIGHEST
F32, BF16 = jnp.float32, jnp.bfloat16

ORB = 32
LX, LY, LZ = 4, 16, 256
NGX, NGY = 32, 8
NXC, NYC, NZC, NC = 4, 4, 8, 2
CH = 4
NCH = ORB // CH
GR = 16
ROWS = ORB * LY

SCALE = 5040.0
SIDE = {1: 8064.0, 2: -1008.0, 3: 128.0, 4: -9.0}
CENTRE = 0.5 * 3.0 * 205.0 / 72.0


def side(distance):
    return SIDE.get(abs(distance), 0.0)


def stencil_matrices():
    own, xl, xr, yl, yr = (np.zeros((LX, LY, LX, LY)) for _ in range(5))
    for x, y, u, v in itertools.product(range(LX), range(LY), range(LX), range(LY)):
        if y == v:
            own[x, y, u, v] += side(x - u)
            xl[x, y, u, v] = side(x - (u - LX))
            xr[x, y, u, v] = side(x - (u + LX))
        if x == u:
            own[x, y, u, v] += side(y - v)
            yl[x, y, u, v] = side(y - (v - LY))
            yr[x, y, u, v] = side(y - (v + LY))
    n = LX * LY
    blocks = [np.kron(np.eye(CH), part.reshape(n, n)) for part in (own, xl, xr, yl, yr)]
    along = np.zeros((LZ, LZ))
    for z in range(LZ):
        for d in (1, 2, 3, 4):
            along[z, (z + d) % LZ] += SIDE[d]
            along[z, (z - d) % LZ] += SIDE[d]
    return np.concatenate(blocks, 1).astype(ml_dtypes.bfloat16), along.astype(ml_dtypes.bfloat16)


def dot(a, b, precision=None):
    return jnp.dot(a, b, preferred_element_type=F32, precision=precision)


def dot_nt(a, b, precision=None):
    return lax.dot_general(a, b, (((1,), (1,)), ((), ())), preferred_element_type=F32, precision=precision)


def ring_distance(d, n):
    return min(d, n - d)


XY_OFFSETS = sorted(
    [o for o in itertools.product(range(NXC), range(NYC)) if o != (0, 0)],
    key=lambda o: -(ring_distance(o[0], NXC) + ring_distance(o[1], NYC)),
)
ZC_OFFSETS = sorted(
    [o for o in itertools.product(range(NZC), range(NC)) if o != (0, 0)],
    key=lambda o: -(ring_distance(o[0], NZC) + 0.5 * o[1]),
)


def kernel(
    occ, sea, pre, occ_im, pre_im, pot, ritz, amat, zmat, rep, rep96,
    nb_out, ritz_out, si_out,
    o_v, s_v, p_v, oi_v, pi_v, v_v, xl, xr, yl, yr, si_v, nb_v, rk, rot, grams, rr, kh, kl,
    c1, c2, e1, e2,
    load_sem, send_sem, recv_sem, out_sem, c1s, c1r, c2s, c2r, e1s, e1r, e2s, e2r,
):
    gx, gy = lax.axis_index("gx"), lax.axis_index("gy")
    z, x, y, core = gx // NXC, lax.rem(gx, NXC), gy // NC, lax.rem(gy, NC)
    xp, xm = lax.rem(gx + 1, NGX), lax.rem(gx + NGX - 1, NGX)
    yp, ym = lax.rem(gy + 1, NGY), lax.rem(gy + NGY - 1, NGY)
    neighbours = [(xp, gy), (xm, gy), (gx, yp), (gx, ym)]

    loads = [
        pltpu.make_async_copy(src, dst, load_sem.at[i])
        for i, (src, dst) in enumerate(
            ((occ, o_v), (sea, s_v), (pre, p_v), (occ_im, oi_v), (pre_im, pi_v), (pot, v_v))
        )
    ]
    for load in loads:
        load.start()

    xy_group = []
    for dx, dy in XY_OFFSETS:
        px, py = lax.rem(x + dx, NXC), lax.rem(y + dy, NYC)
        xy_group.append((px * NYC + py, (z * NXC + px, py * NC + core)))
    zc_group = []
    for dz, dc in ZC_OFFSETS:
        pz, pc = lax.rem(z + dz, NZC), lax.rem(core + dc, NC)
        zc_group.append((pz * NC + pc, (pz * NXC + x, y * NC + pc)))
    xy_me, zc_me = x * NYC + y, z * NC + core

    barrier = pltpu.get_barrier_semaphore()
    others = neighbours + [d for _, d in xy_group] + [d for _, d in zc_group]
    for device in others:
        pl.semaphore_signal(barrier, inc=1, device_id=device, device_id_type=MESH)
    pl.semaphore_wait(barrier, len(others))

    halos = (xl, xr, yl, yr)

    def halo_copy(way, c):
        part = pl.ds(c * CH, CH)
        return pltpu.make_async_remote_copy(
            sea.at[part], halos[way].at[part], send_sem.at[way, c], recv_sem.at[way, c],
            device_id=neighbours[way], device_id_type=MESH,
        )

    for c in range(NCH):
        for way in range(4):
            halo_copy(way, c).start()

    def post(buf, me, group, sends, recvs, value):
        buf[me] = value
        for i, (_, device) in enumerate(group):
            pltpu.make_async_remote_copy(
                buf.at[me], buf.at[me], sends.at[i], recvs.at[me], device_id=device, device_id_type=MESH
            ).start()

    def collect(buf, me, group, sends, recvs):
        for i, (slot, device) in enumerate(group):
            pltpu.make_async_remote_copy(
                buf.at[slot], buf.at[slot], sends.at[i], recvs.at[slot], device_id=device, device_id_type=MESH
            ).wait_recv()
        total = buf[0]
        for slot in range(1, 16):
            total = total + buf[slot]
        return total

    def drain(buf, me, group, sends, recvs):
        for i, (_, device) in enumerate(group):
            pltpu.make_async_remote_copy(
                buf.at[me], buf.at[me], sends.at[i], recvs.at[me], device_id=device, device_id_type=MESH
            ).wait_send()

    def pack(square):
        return jnp.concatenate([square[8 * b : 8 * b + 8, :] for b in range(4)], axis=1)

    def unpack(packed):
        return jnp.concatenate([packed[:, 32 * b : 32 * b + 32] for b in range(4)], axis=0)

    def same_y(width):
        row = lax.broadcasted_iota(jnp.int32, (LY, width), 0)
        column = lax.broadcasted_iota(jnp.int32, (LY, width), 1)
        return jnp.where(row == (column & (LY - 1)), 1.0, 0.0).astype(F32)

    def masked(values):
        width = values.shape[1]
        return values.reshape(-1, LY, width) * same_y(width)[None]

    ritz_cols = dot(ritz[...].astype(F32).T.astype(BF16), rep96[...].T).astype(BF16)
    for block in range(3):
        spread = dot(rep[...], ritz_cols[:, block * ROWS : (block + 1) * ROWS])
        rk[:, block * ROWS : (block + 1) * ROWS] = masked(spread).reshape(ROWS, ROWS).astype(BF16)

    loads[0].wait()
    loads[1].wait()
    loads[2].wait()

    @pl.loop(0, LX)
    def _(i):
        rows = jnp.concatenate([ref[:, i].reshape(ROWS, LZ) for ref in (o_v, s_v, p_v)], axis=0)
        rotated = dot(rk[...], rows)
        high = rotated.astype(BF16)
        columns = pl.ds(pl.multiple_of(i * LZ, LZ), LZ)
        rot[0:ROWS, columns] = high
        rot[ROWS : 2 * ROWS, columns] = (rotated - high.astype(F32)).astype(BF16)

    products = dot_nt(rot[0:ROWS, :], rot[...])
    folded = masked(products).sum(axis=1)
    high_high = dot(folded[:, 0:ROWS], rep[...].astype(F32), HIGHEST)
    high_low = dot(folded[:, ROWS : 2 * ROWS], rep[...].astype(F32), HIGHEST)
    correlation = high_high + high_low + high_low.T
    post(c1, xy_me, xy_group, c1s, c1r, pack(correlation))

    def gram(ref, first):
        rows = jnp.concatenate([ref[first : first + GR, i].reshape(GR * LY, LZ) for i in range(LX)], axis=1)
        products = dot_nt(rot[...], rows)
        return masked(products[0:ROWS] + products[ROWS : 2 * ROWS]).sum(axis=1)

    loads[3].wait()
    grams[:, 0:256] = gram(oi_v, 0)
    grams[:, 256:512] = gram(oi_v, GR)
    post(c2, zc_me, zc_group, c2s, c2r, collect(c1, xy_me, xy_group, c1s, c1r))
    loads[4].wait()
    grams[:, 1024:1280] = gram(pi_v, 0)
    grams[:, 1280:1536] = gram(pi_v, GR)
    correlation = unpack(collect(c2, zc_me, zc_group, c2s, c2r))

    lane = lax.broadcasted_iota(jnp.int32, (ORB, 2 * ORB), 1)
    row = lax.broadcasted_iota(jnp.int32, (ORB, 2 * ORB), 0)
    identity = jnp.where(lane == row + ORB, 1.0, 0.0).astype(F32)
    work = jnp.concatenate([correlation, identity[:, ORB:]], axis=1)
    row_number = lax.broadcasted_iota(jnp.int32, (ORB, 1), 0)
    for k in range(ORB):
        pivot_row = work[k : k + 1, :]
        scaled = pivot_row / work[k : k + 1, k : k + 1]
        column = jnp.where(row_number > k, work[:, k : k + 1], 0.0)
        work = work - column * scaled
    pivots = jnp.sum(jnp.where(lane == row, work, 0.0), axis=1, keepdims=True)
    inverse = work[:, ORB : 2 * ORB] / jnp.sqrt(pivots)

    inverse_high = inverse.astype(BF16)
    inverse_low = (inverse - inverse_high.astype(F32)).astype(BF16)
    for ref, part in ((kh, inverse_high), (kl, inverse_low)):
        spread = dot(rep[...], dot_nt(part, rep[...]).astype(BF16))
        ref[...] = masked(spread).reshape(ROWS, ROWS).astype(BF16)

    @pl.loop(0, LX)
    def _(i):
        columns = pl.ds(pl.multiple_of(i * LZ, LZ), LZ)
        high, low = rot[0:ROWS, columns], rot[ROWS : 2 * ROWS, columns]
        block = dot(kh[...], high) + (dot(kl[...], high) + dot(kh[...], low))
        nb_v[:, i] = block.astype(BF16).reshape(ORB, LY, LZ)

    nb_store = pltpu.make_async_copy(nb_v, nb_out, out_sem.at[NCH])
    nb_store.start()

    ritz_spread = dot(rep96[...], ritz[...])
    rr[...] = dot_nt(ritz_spread, inverse, HIGHEST)

    loads[5].wait()

    def stencil_chunk(c):
        for way in range(4):
            halo_copy(way, c).wait_recv()
        part = pl.ds(c * CH, CH)
        n = CH * LX * LY
        own = s_v[part].reshape(n, LZ)
        rows = jnp.concatenate([own] + [ref[part].reshape(n, LZ) for ref in halos], axis=0)
        summed = dot(amat[...], rows) + dot(own, zmat[...])
        weight = (v_v[...] + CENTRE).reshape(1, LX * LY, LZ)
        image = weight * own.astype(F32).reshape(CH, LX * LY, LZ)
        image = image - (0.5 / SCALE) * summed.reshape(CH, LX * LY, LZ)
        si_v[part] = image.astype(BF16).reshape(CH, LX, LY, LZ)
        pltpu.make_async_copy(si_v.at[part], si_out.at[part], out_sem.at[c]).start()

    @pl.loop(0, NCH // 2)
    def _(c):
        stencil_chunk(c)

    grams[:, 512:768] = gram(si_v, 0)
    early = dot(grams[:, 0:768], rr[0:768, :], HIGHEST) + dot(grams[:, 1024:1536], rr[1024:1536, :], HIGHEST)

    @pl.loop(NCH // 2, NCH)
    def _(c):
        stencil_chunk(c)

    energy = early + dot(gram(si_v, GR), rr[768:1024, :], HIGHEST)
    energy = dot(inverse, energy, HIGHEST)
    post(e1, xy_me, xy_group, e1s, e1r, pack(energy))
    post(e2, zc_me, zc_group, e2s, e2r, collect(e1, xy_me, xy_group, e1s, e1r))

    for way in range(4):
        for c in range(NCH):
            halo_copy(way, c).wait_send()
    for c in range(NCH):
        part = pl.ds(c * CH, CH)
        pltpu.make_async_copy(si_v.at[part], si_out.at[part], out_sem.at[c]).wait()
    nb_store.wait()
    drain(c1, xy_me, xy_group, c1s, c1r)
    drain(c2, zc_me, zc_group, c2s, c2r)
    drain(e1, xy_me, xy_group, e1s, e1r)
    ritz_out[...] = unpack(collect(e2, zc_me, zc_group, e2s, e2r))
    drain(e2, zc_me, zc_group, e2s, e2r)


def per_device(occupied, search_dirs, previous_dirs, occupied_image, previous_image, potential, ritz_vectors):
    amat, zmat = stencil_matrices()
    rep96 = np.kron(np.eye(3 * ORB), np.ones((LY, 1))).astype(ml_dtypes.bfloat16)
    rep = np.kron(np.eye(ORB), np.ones((LY, 1))).astype(ml_dtypes.bfloat16)
    anywhere = pl.BlockSpec(memory_space=pl.ANY)
    vmem = pl.BlockSpec(memory_space=pltpu.VMEM)
    block = (ORB, LX, LY, LZ)
    dma = pltpu.SemaphoreType.DMA
    return pl.pallas_call(
        kernel,
        out_shape=(
            jax.ShapeDtypeStruct(block, BF16),
            jax.ShapeDtypeStruct((ORB, ORB), F32),
            jax.ShapeDtypeStruct(block, BF16),
        ),
        in_specs=[anywhere] * 6 + [vmem] * 5,
        out_specs=(anywhere, vmem, anywhere),
        scratch_shapes=[pltpu.VMEM(block, BF16)] * 5
        + [pltpu.VMEM((LX, LY, LZ), F32)]
        + [pltpu.VMEM(block, BF16)] * 6
        + [
            pltpu.VMEM((ROWS, 3 * ROWS), BF16),
            pltpu.VMEM((2 * ROWS, LX * LZ), BF16),
            pltpu.VMEM((ORB, 3 * ROWS), F32),
            pltpu.VMEM((3 * ROWS, ORB), F32),
            pltpu.VMEM((ROWS, ROWS), BF16),
            pltpu.VMEM((ROWS, ROWS), BF16),
        ]
        + [pltpu.VMEM((16, 8, 128), F32)] * 4
        + [dma((6,)), dma((4, NCH)), dma((4, NCH)), dma((NCH + 1,))]
        + [dma((16,))] * 8,
        compiler_params=pltpu.CompilerParams(
            collective_id=0, has_side_effects=True, vmem_limit_bytes=56 * 2**20
        ),
    )(
        occupied, search_dirs, previous_dirs, occupied_image, previous_image, potential, ritz_vectors,
        jnp.asarray(amat), jnp.asarray(zmat), jnp.asarray(rep), jnp.asarray(rep96),
    )


def solution(mesh):
    cells = P(None, "gx", "gy", None)
    return jax.shard_map(
        per_device,
        mesh=mesh,
        in_specs=(cells, cells, cells, cells, cells, P("gx", "gy", None), P()),
        out_specs=(cells, P(), cells),
        check_vma=False,
    )
```

```python
import itertools

import jax
import jax.numpy as jnp
import ml_dtypes
import numpy as np
from jax import lax
from jax.experimental import pallas as pl
from jax.experimental.pallas import tpu as pltpu
from jax.sharding import PartitionSpec as P

MESH = pl.DeviceIdType.MESH
HIGHEST = lax.Precision.HIGHEST
F32, BF16 = jnp.float32, jnp.bfloat16

ORB = 32
LX, LY, LZ = 4, 16, 256
NGX, NGY = 32, 8
NXC, NYC, NZC, NC = 4, 4, 8, 2
SENT = (3, 6)
EARLY = 1
CH = 4
NCH = ORB // CH
GR = 16
ROWS = ORB * LY

SCALE = 5040.0
SIDE = {1: 8064.0, 2: -1008.0, 3: 128.0, 4: -9.0}
CENTRE = 0.5 * 3.0 * 205.0 / 72.0


def side(distance):
    return SIDE.get(abs(distance), 0.0)


def lane_blocks(matrix):
    return np.concatenate(np.split(matrix, matrix.shape[1] // 128, axis=1), 0).astype(ml_dtypes.bfloat16)


def side_by_side(ref, rows):
    return jnp.concatenate([ref[first : first + rows] for first in range(0, ref.shape[0], rows)], axis=1)


def stencil_matrices():
    own, xl, xr, yl, yr = (np.zeros((LX, LY, LX, LY)) for _ in range(5))
    for x, y, u, v in itertools.product(range(LX), range(LY), range(LX), range(LY)):
        if y == v:
            own[x, y, u, v] += side(x - u)
            xl[x, y, u, v] = side(x - (u - LX))
            xr[x, y, u, v] = side(x - (u + LX))
        if x == u:
            own[x, y, u, v] += side(y - v)
            yl[x, y, u, v] = side(y - (v - LY))
            yr[x, y, u, v] = side(y - (v + LY))
    n = LX * LY
    blocks = [np.kron(np.eye(CH), part.reshape(n, n)) for part in (own, xl, xr, yl, yr)]
    along = np.zeros((LZ, LZ))
    for z in range(LZ):
        for d in (1, 2, 3, 4):
            along[z, (z + d) % LZ] += SIDE[d]
            along[z, (z - d) % LZ] += SIDE[d]
    return lane_blocks(np.concatenate(blocks, 1)), lane_blocks(along)


def dot(a, b, precision=None):
    return jnp.dot(a, b, preferred_element_type=F32, precision=precision)


def dot_nt(a, b, precision=None):
    return lax.dot_general(a, b, (((1,), (1,)), ((), ())), preferred_element_type=F32, precision=precision)


def dot_split(a, b):
    first = a.astype(BF16)
    rest = a - first.astype(F32)
    second = rest.astype(BF16)
    third = (rest - second.astype(F32)).astype(BF16)
    n = a.shape[0]
    parts = dot(jnp.concatenate([first, second, third], axis=0), b)
    return parts[0:n] + (parts[n : 2 * n] + parts[2 * n : 3 * n])


def ring_distance(d, n):
    return min(d, n - d)


XY_OFFSETS = sorted(
    [o for o in itertools.product(range(NXC), range(NYC)) if o != (0, 0)],
    key=lambda o: -(ring_distance(o[0], NXC) + ring_distance(o[1], NYC)),
)
ZC_OFFSETS = sorted(
    [o for o in itertools.product(range(NZC), range(NC)) if o != (0, 0)],
    key=lambda o: -(ring_distance(o[0], NZC) + 0.5 * o[1]),
)


def kernel(
    occ, sea, pre, occ_im, pre_im, pot, ritz_in, amat_in, zmat_in, rep_in, rep96_in,
    nb_v, ritz_out, si_v,
    o_v, s_v, p_v, oi_v, pi_v, v_v, xl, xr, yl, yr, rk, rot, grams, kh, kl, ritz, amat, zmat, rep, rep96,
    c1, c2, e1, e2,
    load_sem, send_sem, recv_sem, c1s, c1r, c2s, c2r, e1s, e1r, e2s, e2r,
):
    gx, gy = lax.axis_index("gx"), lax.axis_index("gy")
    z, x, y, core = gx // NXC, lax.rem(gx, NXC), gy // NC, lax.rem(gy, NC)
    xp, xm = lax.rem(gx + 1, NGX), lax.rem(gx + NGX - 1, NGX)
    yp, ym = lax.rem(gy + 1, NGY), lax.rem(gy + NGY - 1, NGY)
    neighbours = [(xp, gy), (xm, gy), (gx, yp), (gx, ym)]

    loads = [
        pltpu.make_async_copy(src, dst, load_sem.at[i])
        for i, (src, dst) in enumerate(
            (
                (ritz_in, ritz), (rep96_in, rep96), (rep_in, rep), (occ, o_v), (sea, s_v), (pre, p_v),
                (occ_im, oi_v), (pre_im, pi_v), (pot, v_v), (amat_in, amat), (zmat_in, zmat),
            )
        )
    ]

    xy_group = []
    for dx, dy in XY_OFFSETS:
        px, py = lax.rem(x + dx, NXC), lax.rem(y + dy, NYC)
        xy_group.append((px * NYC + py, (z * NXC + px, py * NC + core)))
    zc_group = []
    for dz, dc in ZC_OFFSETS:
        pz, pc = lax.rem(z + dz, NZC), lax.rem(core + dc, NC)
        zc_group.append((pz * NC + pc, (pz * NXC + x, y * NC + pc)))
    xy_me, zc_me = x * NYC + y, z * NC + core

    barrier = pltpu.get_barrier_semaphore()
    others = neighbours + [d for _, d in xy_group] + [d for _, d in zc_group]
    for device in others:
        pl.semaphore_signal(barrier, inc=1, device_id=device, device_id_type=MESH)
    pl.semaphore_wait(barrier, len(others))

    halos = (xl, xr, yl, yr)

    def halo_copy(way, c):
        part = pl.ds(c * CH, CH)
        return pltpu.make_async_remote_copy(
            sea.at[part], halos[way].at[part], send_sem.at[way, c], recv_sem.at[way, c],
            device_id=neighbours[way], device_id_type=MESH,
        )

    def send_chunks(first, last):
        for c in range(first, last):
            for way in range(4):
                halo_copy(way, c).start()

    send_chunks(0, 1)
    for load in loads:
        load.start()
    send_chunks(1, SENT[0])

    def post(buf, me, group, sends, recvs, value):
        buf[me] = value
        for i, (_, device) in enumerate(group):
            pltpu.make_async_remote_copy(
                buf.at[me], buf.at[me], sends.at[i], recvs.at[me], device_id=device, device_id_type=MESH
            ).start()

    def collect(buf, me, group, sends, recvs):
        for i, (slot, device) in enumerate(group):
            pltpu.make_async_remote_copy(
                buf.at[slot], buf.at[slot], sends.at[i], recvs.at[slot], device_id=device, device_id_type=MESH
            ).wait_recv()
        total = buf[0]
        for slot in range(1, 16):
            total = total + buf[slot]
        return total

    def drain(buf, me, group, sends, recvs):
        for i, (_, device) in enumerate(group):
            pltpu.make_async_remote_copy(
                buf.at[me], buf.at[me], sends.at[i], recvs.at[me], device_id=device, device_id_type=MESH
            ).wait_send()

    def pack(square):
        return jnp.concatenate([square[8 * b : 8 * b + 8, :] for b in range(4)], axis=1)

    def unpack(packed):
        return jnp.concatenate([packed[:, 32 * b : 32 * b + 32] for b in range(4)], axis=0)

    def same_y(width):
        row = lax.broadcasted_iota(jnp.int32, (LY, width), 0)
        column = lax.broadcasted_iota(jnp.int32, (LY, width), 1)
        return jnp.where(row == (column & (LY - 1)), 1.0, 0.0).astype(F32)

    def masked(values):
        width = values.shape[1]
        return values.reshape(-1, LY, width) * same_y(width)[None]

    for load in loads[:3]:
        load.wait()

    ritz_cols = dot_nt(ritz[...], rep96[...]).astype(BF16)
    for block in range(3):
        spread = dot(rep[...], ritz_cols[:, block * ROWS : (block + 1) * ROWS])
        rk[:, block * ROWS : (block + 1) * ROWS] = masked(spread).reshape(ROWS, ROWS).astype(BF16)
    ritz_rows = dot_nt(rep96[...], ritz[...]).astype(BF16)

    for load in loads[3:6]:
        load.wait()

    @pl.loop(0, LX)
    def _(i):
        rows = jnp.concatenate([ref[:, i].reshape(ROWS, LZ) for ref in (o_v, s_v, p_v)], axis=0)
        rotated = dot(rk[...], rows)
        high = rotated.astype(BF16)
        columns = pl.ds(pl.multiple_of(i * LZ, LZ), LZ)
        rot[0:ROWS, columns] = high
        rot[ROWS : 2 * ROWS, columns] = (rotated - high.astype(F32)).astype(BF16)

    products = dot_nt(rot[0:ROWS, :], rot[...])
    folded = masked(products).sum(axis=1)
    high_high = dot_split(folded[:, 0:ROWS], rep[...])
    high_low = dot_split(folded[:, ROWS : 2 * ROWS], rep[...])
    correlation = high_high + high_low + high_low.T
    post(c1, zc_me, zc_group, c1s, c1r, pack(correlation))
    send_chunks(SENT[0], SENT[1])

    def gram(ref, first):
        rows = jnp.concatenate([ref[first : first + GR, i].reshape(GR * LY, LZ) for i in range(LX)], axis=1)
        products = dot_nt(rot[...], rows)
        return masked(products[0:ROWS] + products[ROWS : 2 * ROWS]).sum(axis=1)

    for load in loads[8:]:
        load.wait()

    def stencil_chunk(c):
        for way in range(4):
            halo_copy(way, c).wait_recv()
        part = pl.ds(c * CH, CH)
        n = CH * LX * LY
        own = s_v[part].reshape(n, LZ)
        rows = jnp.concatenate([own] + [ref[part].reshape(n, LZ) for ref in halos], axis=0)
        summed = dot(side_by_side(amat, n), rows) + dot(own, side_by_side(zmat, LZ))
        weight = (v_v[...] + CENTRE).reshape(1, LX * LY, LZ)
        image = weight * own.astype(F32).reshape(CH, LX * LY, LZ)
        image = image - (0.5 / SCALE) * summed.reshape(CH, LX * LY, LZ)
        si_v[part] = image.astype(BF16).reshape(CH, LX, LY, LZ)

    loads[6].wait()
    grams[:, 0:256] = gram(oi_v, 0)
    grams[:, 256:512] = gram(oi_v, GR)
    loads[7].wait()
    grams[:, 768:1024] = gram(pi_v, 0)
    grams[:, 1024:1280] = gram(pi_v, GR)

    @pl.loop(0, EARLY)
    def _(c):
        stencil_chunk(c)

    post(c2, xy_me, xy_group, c2s, c2r, collect(c1, zc_me, zc_group, c1s, c1r))
    send_chunks(SENT[1], NCH)

    @pl.loop(EARLY, NCH // 2)
    def _(c):
        stencil_chunk(c)

    grams[:, 512:768] = gram(si_v, 0)
    early = dot_split(grams[:, 0:768], ritz_rows[0:768]) + dot_split(grams[:, 768:1280], ritz_rows[1024:1536])

    @pl.loop(NCH // 2, NCH)
    def _(c):
        stencil_chunk(c)

    energy = early + dot_split(gram(si_v, GR), ritz_rows[768:1024])
    post(e1, xy_me, xy_group, e1s, e1r, pack(energy))

    correlation = unpack(collect(c2, xy_me, xy_group, c2s, c2r))

    lane = lax.broadcasted_iota(jnp.int32, (ORB, 2 * ORB), 1)
    row = lax.broadcasted_iota(jnp.int32, (ORB, 2 * ORB), 0)
    identity = jnp.where(lane == row + ORB, 1.0, 0.0).astype(F32)
    work = jnp.concatenate([correlation, identity[:, ORB:]], axis=1)
    row_number = lax.broadcasted_iota(jnp.int32, (ORB, 1), 0)
    for k in range(ORB):
        pivot_row = work[k : k + 1, :]
        scaled = pivot_row / work[k : k + 1, k : k + 1]
        column = jnp.where(row_number > k, work[:, k : k + 1], 0.0)
        work = work - column * scaled
    pivots = jnp.sum(jnp.where(lane == row, work, 0.0), axis=1, keepdims=True)
    inverse = work[:, ORB : 2 * ORB] / jnp.sqrt(pivots)

    inverse_high = inverse.astype(BF16)
    inverse_low = (inverse - inverse_high.astype(F32)).astype(BF16)
    for ref, part in ((kh, inverse_high), (kl, inverse_low)):
        spread = dot(rep[...], dot_nt(part, rep[...]).astype(BF16))
        ref[...] = masked(spread).reshape(ROWS, ROWS).astype(BF16)

    post(e2, zc_me, zc_group, e2s, e2r, collect(e1, xy_me, xy_group, e1s, e1r))

    def rotate(i):
        columns = pl.ds(pl.multiple_of(i * LZ, LZ), LZ)
        high, low = rot[0:ROWS, columns], rot[ROWS : 2 * ROWS, columns]
        block = dot(kh[...], high) + (dot(kl[...], high) + dot(kh[...], low))
        nb_v[:, i] = block.astype(BF16).reshape(ORB, LY, LZ)

    @pl.loop(0, LX)
    def _(i):
        rotate(i)

    for way in range(4):
        for c in range(NCH):
            halo_copy(way, c).wait_send()
    drain(c1, zc_me, zc_group, c1s, c1r)
    drain(c2, xy_me, xy_group, c2s, c2r)
    drain(e1, xy_me, xy_group, e1s, e1r)
    energy = unpack(collect(e2, zc_me, zc_group, e2s, e2r))
    ritz_out[...] = dot_nt(dot(inverse, energy, HIGHEST), inverse, HIGHEST)
    drain(e2, zc_me, zc_group, e2s, e2r)


def hand_over(nb_v, ritz_v, si_v, nb_out, ritz_out, si_out, sems):
    copies = [
        pltpu.make_async_copy(src, dst, sems.at[i])
        for i, (src, dst) in enumerate(((nb_v, nb_out), (si_v, si_out), (ritz_v, ritz_out)))
    ]
    for copy in copies:
        copy.start()
    for copy in copies:
        copy.wait()


def per_device(occupied, search_dirs, previous_dirs, occupied_image, previous_image, potential, ritz_vectors):
    amat, zmat = stencil_matrices()
    rep96 = np.kron(np.eye(3 * ORB), np.ones((LY, 1))).astype(ml_dtypes.bfloat16)
    rep = np.kron(np.eye(ORB), np.ones((LY, 1))).astype(ml_dtypes.bfloat16)
    anywhere = pl.BlockSpec(memory_space=pl.ANY)
    vmem = pl.BlockSpec(memory_space=pltpu.VMEM)
    block = (ORB, LX, LY, LZ)
    dma = pltpu.SemaphoreType.DMA
    results = pl.pallas_call(
        kernel,
        out_shape=(pltpu.VMEM(block, BF16), pltpu.VMEM((ORB, ORB), F32), pltpu.VMEM(block, BF16)),
        in_specs=[pl.BlockSpec(memory_space=pltpu.HBM)] * 11,
        out_specs=(vmem, vmem, vmem),
        scratch_shapes=[pltpu.VMEM(block, BF16)] * 5
        + [pltpu.VMEM((LX, LY, LZ), F32)]
        + [pltpu.VMEM(block, BF16)] * 4
        + [
            pltpu.VMEM((ROWS, 3 * ROWS), BF16),
            pltpu.VMEM((2 * ROWS, LX * LZ), BF16),
            pltpu.VMEM((ORB, 5 * GR * LY), F32),
            pltpu.VMEM((ROWS, ROWS), BF16),
            pltpu.VMEM((ROWS, ROWS), BF16),
            pltpu.VMEM((ORB, 3 * ORB), BF16),
            pltpu.VMEM(amat.shape, BF16),
            pltpu.VMEM(zmat.shape, BF16),
            pltpu.VMEM(rep.shape, BF16),
            pltpu.VMEM(rep96.shape, BF16),
        ]
        + [pltpu.VMEM((16, 8, 128), F32)] * 4
        + [dma((11,)), dma((4, NCH)), dma((4, NCH))]
        + [dma((16,))] * 8,
        compiler_params=pltpu.CompilerParams(
            collective_id=0, has_side_effects=True, vmem_limit_bytes=52 * 2**20
        ),
    )(
        occupied, search_dirs, previous_dirs, occupied_image, previous_image, potential, ritz_vectors.T,
        jnp.asarray(amat), jnp.asarray(zmat), jnp.asarray(rep), jnp.asarray(rep96),
    )
    return pl.pallas_call(
        hand_over,
        out_shape=(
            jax.ShapeDtypeStruct(block, BF16),
            jax.ShapeDtypeStruct((ORB, ORB), F32),
            jax.ShapeDtypeStruct(block, BF16),
        ),
        in_specs=[vmem, vmem, vmem],
        out_specs=(anywhere, anywhere, anywhere),
        scratch_shapes=[dma((3,))],
        compiler_params=pltpu.CompilerParams(vmem_limit_bytes=2**20),
    )(*[pltpu.with_memory_space_constraint(result, pltpu.VMEM) for result in results])


def solution(mesh):
    cells = P(None, "gx", "gy", None)
    return jax.shard_map(
        per_device,
        mesh=mesh,
        in_specs=(cells, cells, cells, cells, cells, P("gx", "gy", None), P()),
        out_specs=(cells, P(), cells),
        check_vma=False,
    )
```

```python
import itertools

import jax
import jax.numpy as jnp
import ml_dtypes
import numpy as np
from jax import lax
from jax.experimental import pallas as pl
from jax.experimental.pallas import tpu as pltpu
from jax.sharding import PartitionSpec as P

MESH = pl.DeviceIdType.MESH
HIGHEST = lax.Precision.HIGHEST
F32, BF16 = jnp.float32, jnp.bfloat16

ORB = 32
LX, LY, LZ = 4, 16, 256
NGX, NGY = 32, 8
NXC, NYC, NZC, NC = 4, 4, 8, 2
SENT = 3
PIECES = 1
SLOTS = (NC, NZC, NYC, NXC, NXC * NYC, NZC * NC)
EARLY = 1
CH = 4
NCH = ORB // CH
GR = 16
ROWS = ORB * LY

SCALE = 5040.0
SIDE = {1: 8064.0, 2: -1008.0, 3: 128.0, 4: -9.0}
CENTRE = 0.5 * 3.0 * 205.0 / 72.0


def side(distance):
    return SIDE.get(abs(distance), 0.0)


def lane_blocks(matrix):
    return np.concatenate(np.split(matrix, matrix.shape[1] // 128, axis=1), 0).astype(ml_dtypes.bfloat16)


def side_by_side(ref, rows):
    return jnp.concatenate([ref[first : first + rows] for first in range(0, ref.shape[0], rows)], axis=1)


def stencil_matrices():
    own, xl, xr, yl, yr = (np.zeros((LX, LY, LX, LY)) for _ in range(5))
    for x, y, u, v in itertools.product(range(LX), range(LY), range(LX), range(LY)):
        if y == v:
            own[x, y, u, v] += side(x - u)
            xl[x, y, u, v] = side(x - (u - LX))
            xr[x, y, u, v] = side(x - (u + LX))
        if x == u:
            own[x, y, u, v] += side(y - v)
            yl[x, y, u, v] = side(y - (v - LY))
            yr[x, y, u, v] = side(y - (v + LY))
    n = LX * LY
    blocks = [np.kron(np.eye(CH), part.reshape(n, n)) for part in (own, xl, xr, yl, yr)]
    along = np.zeros((LZ, LZ))
    for z in range(LZ):
        for d in (1, 2, 3, 4):
            along[z, (z + d) % LZ] += SIDE[d]
            along[z, (z - d) % LZ] += SIDE[d]
    return lane_blocks(np.concatenate(blocks, 1)), lane_blocks(along)


def dot(a, b, precision=None):
    return jnp.dot(a, b, preferred_element_type=F32, precision=precision)


def dot_nt(a, b, precision=None):
    return lax.dot_general(a, b, (((1,), (1,)), ((), ())), preferred_element_type=F32, precision=precision)


def dot_split(a, b):
    first = a.astype(BF16)
    rest = a - first.astype(F32)
    second = rest.astype(BF16)
    third = (rest - second.astype(F32)).astype(BF16)
    n = a.shape[0]
    parts = dot(jnp.concatenate([first, second, third], axis=0), b)
    return parts[0:n] + (parts[n : 2 * n] + parts[2 * n : 3 * n])


def ring_distance(d, n):
    return min(d, n - d)


XY_OFFSETS = sorted(
    [o for o in itertools.product(range(NXC), range(NYC)) if o != (0, 0)],
    key=lambda o: -(ring_distance(o[0], NXC) + ring_distance(o[1], NYC)),
)
ZC_OFFSETS = sorted(
    [o for o in itertools.product(range(NZC), range(NC)) if o != (0, 0)],
    key=lambda o: -(ring_distance(o[0], NZC) + 0.5 * o[1]),
)
Z_OFFSETS = sorted(range(1, NZC), key=lambda d: -ring_distance(d, NZC))


def kernel(
    occ, sea, pre, occ_im, pre_im, pot, ritz_in, amat_in, zmat_in, rep_in, rep96_in,
    nb_v, ritz_out, si_v,
    o_v, s_v, p_v, oi_v, pi_v, v_v, xl, xr, yl, yr, rk, rot, grams, kh, kl, ritz, amat, zmat, rep, rep96,
    c0, c1, c2, c3, e1, e2,
    load_sem, send_sem, recv_sem, c0s, c0r, c1s, c1r, c2s, c2r, c3s, c3r, e1s, e1r, e2s, e2r,
):
    gx, gy = lax.axis_index("gx"), lax.axis_index("gy")
    z, x, y, core = gx // NXC, lax.rem(gx, NXC), gy // NC, lax.rem(gy, NC)
    xp, xm = lax.rem(gx + 1, NGX), lax.rem(gx + NGX - 1, NGX)
    yp, ym = lax.rem(gy + 1, NGY), lax.rem(gy + NGY - 1, NGY)
    neighbours = [(xp, gy), (xm, gy), (gx, yp), (gx, ym)]

    loads = [
        pltpu.make_async_copy(src, dst, load_sem.at[i])
        for i, (src, dst) in enumerate(
            (
                (ritz_in, ritz), (rep96_in, rep96), (rep_in, rep), (occ, o_v), (sea, s_v), (pre, p_v),
                (occ_im, oi_v), (pre_im, pi_v), (pot, v_v), (amat_in, amat), (zmat_in, zmat),
            )
        )
    ]

    xy_group = []
    for dx, dy in XY_OFFSETS:
        px, py = lax.rem(x + dx, NXC), lax.rem(y + dy, NYC)
        xy_group.append((px * NYC + py, (z * NXC + px, py * NC + core)))
    z_group = []
    for dz in Z_OFFSETS:
        pz = lax.rem(z + dz, NZC)
        z_group.append((pz, (pz * NXC + x, gy)))
    pair = [(1 - core, (gx, y * NC + 1 - core))]
    zc_group = []
    for dz, dc in ZC_OFFSETS:
        pz, pc = lax.rem(z + dz, NZC), lax.rem(core + dc, NC)
        zc_group.append((pz * NC + pc, (pz * NXC + x, y * NC + pc)))
    xy_me, zc_me = x * NYC + y, z * NC + core
    x_group = [(lax.rem(x + d, NXC), (z * NXC + lax.rem(x + d, NXC), gy)) for d in (2, 1, 3)]
    y_group = [(lax.rem(y + d, NYC), (gx, lax.rem(y + d, NYC) * NC + core)) for d in (2, 1, 3)]

    barrier = pltpu.get_barrier_semaphore()
    others = neighbours + [d for _, d in xy_group + zc_group]
    for device in others:
        pl.semaphore_signal(barrier, inc=1, device_id=device, device_id_type=MESH)
    pl.semaphore_wait(barrier, len(others))

    halos = (xl, xr, yl, yr)

    def halo_copy(way, c):
        part = pl.ds(c * CH, CH)
        return pltpu.make_async_remote_copy(
            sea.at[part], halos[way].at[part], send_sem.at[way, c], recv_sem.at[way, c],
            device_id=neighbours[way], device_id_type=MESH,
        )

    def send_chunks(first, last):
        for c in range(first, last):
            for way in range(4):
                halo_copy(way, c).start()

    send_chunks(0, 1)
    for load in loads:
        load.start()
    send_chunks(1, SENT)

    def post(buf, me, group, sends, recvs, value):
        buf[me] = value
        for i, (_, device) in enumerate(group):
            pltpu.make_async_remote_copy(
                buf.at[me], buf.at[me], sends.at[i], recvs.at[me], device_id=device, device_id_type=MESH
            ).start()

    def collect(buf, me, group, sends, recvs):
        for i, (slot, device) in enumerate(group):
            pltpu.make_async_remote_copy(
                buf.at[slot], buf.at[slot], sends.at[i], recvs.at[slot], device_id=device, device_id_type=MESH
            ).wait_recv()
        total = buf[0]
        for slot in range(1, buf.shape[0]):
            total = total + buf[slot]
        return total

    def drain(buf, me, group, sends, recvs):
        for i, (_, device) in enumerate(group):
            pltpu.make_async_remote_copy(
                buf.at[me], buf.at[me], sends.at[i], recvs.at[me], device_id=device, device_id_type=MESH
            ).wait_send()

    def pack(square):
        return jnp.concatenate([square[8 * b : 8 * b + 8, :] for b in range(4)], axis=1)

    def unpack(packed):
        return jnp.concatenate([packed[:, 32 * b : 32 * b + 32] for b in range(4)], axis=0)

    def same_y(width):
        row = lax.broadcasted_iota(jnp.int32, (LY, width), 0)
        column = lax.broadcasted_iota(jnp.int32, (LY, width), 1)
        return jnp.where(row == (column & (LY - 1)), 1.0, 0.0).astype(F32)

    def masked(values):
        width = values.shape[1]
        return values.reshape(-1, LY, width) * same_y(width)[None]

    for load in loads[:3]:
        load.wait()

    ritz_cols = dot_nt(ritz[...], rep96[...]).astype(BF16)
    for block in range(3):
        spread = dot(rep[...], ritz_cols[:, block * ROWS : (block + 1) * ROWS])
        rk[:, block * ROWS : (block + 1) * ROWS] = masked(spread).reshape(ROWS, ROWS).astype(BF16)
    ritz_rows = dot_nt(rep96[...], ritz[...]).astype(BF16)

    for load in loads[3:6]:
        load.wait()

    @pl.loop(0, LX)
    def _(i):
        rows = jnp.concatenate([ref[:, i].reshape(ROWS, LZ) for ref in (o_v, s_v, p_v)], axis=0)
        rotated = dot(rk[...], rows)
        high = rotated.astype(BF16)
        columns = pl.ds(pl.multiple_of(i * LZ, LZ), LZ)
        rot[0:ROWS, columns] = high
        rot[ROWS : 2 * ROWS, columns] = (rotated - high.astype(F32)).astype(BF16)

    products = dot_nt(rot[0:ROWS, :], rot[...])
    folded = masked(products).sum(axis=1)
    high_high = dot_split(folded[:, 0:ROWS], rep[...])
    high_low = dot_split(folded[:, ROWS : 2 * ROWS], rep[...])
    correlation = high_high + high_low + high_low.T
    post(c0, core, pair, c0s, c0r, pack(correlation))

    def gram(ref, first, count=GR):
        rows = jnp.concatenate([ref[first : first + count, i].reshape(count * LY, LZ) for i in range(LX)], axis=1)
        products = dot_nt(rot[...], rows)
        return masked(products[0:ROWS] + products[ROWS : 2 * ROWS]).sum(axis=1)

    for load in loads[8:]:
        load.wait()

    def stencil_chunk(c):
        for way in range(4):
            halo_copy(way, c).wait_recv()
        part = pl.ds(c * CH, CH)
        n = CH * LX * LY
        own = s_v[part].reshape(n, LZ)
        rows = jnp.concatenate([own] + [ref[part].reshape(n, LZ) for ref in halos], axis=0)
        summed = dot(side_by_side(amat, n), rows) + dot(own, side_by_side(zmat, LZ))
        weight = (v_v[...] + CENTRE).reshape(1, LX * LY, LZ)
        image = weight * own.astype(F32).reshape(CH, LX * LY, LZ)
        image = image - (0.5 / SCALE) * summed.reshape(CH, LX * LY, LZ)
        si_v[part] = image.astype(BF16).reshape(CH, LX, LY, LZ)

    loads[6].wait()
    grams[:, 0:256] = gram(oi_v, 0)
    grams[:, 256:512] = gram(oi_v, GR)
    post(c1, z, z_group, c1s, c1r, collect(c0, core, pair, c0s, c0r))
    send_chunks(SENT, NCH)
    loads[7].wait()
    grams[:, 768:1024] = gram(pi_v, 0)
    grams[:, 1024:1280] = gram(pi_v, GR)

    @pl.loop(0, EARLY)
    def _(c):
        stencil_chunk(c)

    post(c2, y, y_group, c2s, c2r, collect(c1, z, z_group, c1s, c1r))

    @pl.loop(EARLY, NCH // 2)
    def _(c):
        stencil_chunk(c)

    grams[:, 512:768] = gram(si_v, 0)
    early = dot_split(grams[:, 0:768], ritz_rows[0:768]) + dot_split(grams[:, 768:1280], ritz_rows[1024:1536])

    post(c3, x, x_group, c3s, c3r, collect(c2, y, y_group, c2s, c2r))

    @pl.loop(NCH // 2, NCH - 1)
    def _(c):
        stencil_chunk(c)

    grams[:, 1280:1472] = gram(si_v, GR, GR - CH)
    early = early + dot_split(grams[:, 1280:1472], ritz_rows[768:960])

    @pl.loop(NCH - 1, NCH)
    def _(c):
        stencil_chunk(c)

    energy = early + dot_split(gram(si_v, ORB - CH, CH), ritz_rows[960:1024])
    post(e1, xy_me, xy_group, e1s, e1r, pack(energy))

    post(e2, zc_me, zc_group, e2s, e2r, collect(e1, xy_me, xy_group, e1s, e1r))

    correlation = unpack(collect(c3, x, x_group, c3s, c3r))

    lane = lax.broadcasted_iota(jnp.int32, (ORB, 2 * ORB), 1)
    row = lax.broadcasted_iota(jnp.int32, (ORB, 2 * ORB), 0)
    identity = jnp.where(lane == row + ORB, 1.0, 0.0).astype(F32)
    work = jnp.concatenate([correlation, identity[:, ORB:]], axis=1)
    row_number = lax.broadcasted_iota(jnp.int32, (ORB, 1), 0)
    for k in range(ORB):
        pivot_row = work[k : k + 1, :]
        scaled = pivot_row / work[k : k + 1, k : k + 1]
        column = jnp.where(row_number > k, work[:, k : k + 1], 0.0)
        work = work - column * scaled
    pivots = jnp.sum(jnp.where(lane == row, work, 0.0), axis=1, keepdims=True)
    inverse = work[:, ORB : 2 * ORB] / jnp.sqrt(pivots)

    inverse_high = inverse.astype(BF16)
    inverse_low = (inverse - inverse_high.astype(F32)).astype(BF16)
    for ref, part in ((kh, inverse_high), (kl, inverse_low)):
        spread = dot(rep[...], dot_nt(part, rep[...]).astype(BF16))
        ref[...] = masked(spread).reshape(ROWS, ROWS).astype(BF16)

    def rotate(i):
        columns = pl.ds(pl.multiple_of(i * LZ, LZ), LZ)
        high, low = rot[0:ROWS, columns], rot[ROWS : 2 * ROWS, columns]
        block = dot(kh[...], high) + (dot(kl[...], high) + dot(kh[...], low))
        nb_v[:, i] = block.astype(BF16).reshape(ORB, LY, LZ)

    @pl.loop(0, LX)
    def _(i):
        rotate(i)

    for way in range(4):
        for c in range(NCH):
            halo_copy(way, c).wait_send()
    drain(c0, core, pair, c0s, c0r)
    drain(c1, z, z_group, c1s, c1r)
    drain(c2, y, y_group, c2s, c2r)
    drain(c3, x, x_group, c3s, c3r)
    drain(e1, xy_me, xy_group, e1s, e1r)
    energy = unpack(collect(e2, zc_me, zc_group, e2s, e2r))
    ritz_out[...] = dot_nt(dot(inverse, energy, HIGHEST), inverse, HIGHEST)
    drain(e2, zc_me, zc_group, e2s, e2r)


def hand_over(nb_v, ritz_v, si_v, nb_out, ritz_out, si_out, sems):
    pairs = [(ritz_v, ritz_out)]
    for first in range(0, ORB, ORB // PIECES):
        part = pl.ds(first, ORB // PIECES)
        pairs += [(nb_v.at[part], nb_out.at[part]), (si_v.at[part], si_out.at[part])]
    copies = [pltpu.make_async_copy(src, dst, sems.at[i]) for i, (src, dst) in enumerate(pairs)]
    for copy in copies:
        copy.start()
    for copy in copies:
        copy.wait()


def per_device(occupied, search_dirs, previous_dirs, occupied_image, previous_image, potential, ritz_vectors):
    amat, zmat = stencil_matrices()
    rep96 = np.kron(np.eye(3 * ORB), np.ones((LY, 1))).astype(ml_dtypes.bfloat16)
    rep = np.kron(np.eye(ORB), np.ones((LY, 1))).astype(ml_dtypes.bfloat16)
    anywhere = pl.BlockSpec(memory_space=pl.ANY)
    vmem = pl.BlockSpec(memory_space=pltpu.VMEM)
    block = (ORB, LX, LY, LZ)
    dma = pltpu.SemaphoreType.DMA
    results = pl.pallas_call(
        kernel,
        out_shape=(pltpu.VMEM(block, BF16), pltpu.VMEM((ORB, ORB), F32), pltpu.VMEM(block, BF16)),
        in_specs=[pl.BlockSpec(memory_space=pltpu.HBM)] * 11,
        out_specs=(vmem, vmem, vmem),
        scratch_shapes=[pltpu.VMEM(block, BF16)] * 5
        + [pltpu.VMEM((LX, LY, LZ), F32)]
        + [pltpu.VMEM(block, BF16)] * 4
        + [
            pltpu.VMEM((ROWS, 3 * ROWS), BF16),
            pltpu.VMEM((2 * ROWS, LX * LZ), BF16),
            pltpu.VMEM((ORB, 6 * GR * LY), F32),
            pltpu.VMEM((ROWS, ROWS), BF16),
            pltpu.VMEM((ROWS, ROWS), BF16),
            pltpu.VMEM((ORB, 3 * ORB), BF16),
            pltpu.VMEM(amat.shape, BF16),
            pltpu.VMEM(zmat.shape, BF16),
            pltpu.VMEM(rep.shape, BF16),
            pltpu.VMEM(rep96.shape, BF16),
        ]
        + [pltpu.VMEM((n, 8, 128), F32) for n in SLOTS]
        + [dma((11,)), dma((4, NCH)), dma((4, NCH))]
        + [dma((n,)) for n in SLOTS for _ in range(2)],
        compiler_params=pltpu.CompilerParams(
            collective_id=0, has_side_effects=True, vmem_limit_bytes=52 * 2**20
        ),
    )(
        occupied, search_dirs, previous_dirs, occupied_image, previous_image, potential, ritz_vectors.T,
        jnp.asarray(amat), jnp.asarray(zmat), jnp.asarray(rep), jnp.asarray(rep96),
    )
    return pl.pallas_call(
        hand_over,
        out_shape=(
            jax.ShapeDtypeStruct(block, BF16),
            jax.ShapeDtypeStruct((ORB, ORB), F32),
            jax.ShapeDtypeStruct(block, BF16),
        ),
        in_specs=[vmem, vmem, vmem],
        out_specs=(anywhere, anywhere, anywhere),
        scratch_shapes=[dma((1 + 2 * PIECES,))],
        compiler_params=pltpu.CompilerParams(vmem_limit_bytes=2**20),
    )(*[pltpu.with_memory_space_constraint(result, pltpu.VMEM) for result in results])


def solution(mesh):
    cells = P(None, "gx", "gy", None)
    return jax.shard_map(
        per_device,
        mesh=mesh,
        in_specs=(cells, cells, cells, cells, cells, P("gx", "gy", None), P()),
        out_specs=(cells, P(), cells),
        check_vma=False,
    )
```
